32 devices in a mesh: chain: 2 (over x), ang: 4 (over y, core), dist: 4 (over z).
Axes of the slice: x: 2, y: 2, z: 4, core: 2. Of those that a mesh axis runs over, the one named last changes fastest.
Arguments:
- latent: float32 [1024, 512, 512], P(('chain', 'dist'), 'ang'), parts along dimension 0, may hold values from -6 to 6
- row_factor: bfloat16 [512, 512], replicated, may hold values from -0.25 to 0.25
- col_factor: bfloat16 [512, 512], replicated, may hold values from -0.25 to 0.25
- log_mean: float32 [1024], P(('chain', 'dist')), parts along dimension 0, may hold values from -6 to -4
- band_ratio: float32 [8], replicated, may hold values from 0.2 to 2
- star_counts: int32 [32, 16], P(('chain', 'ang', 'dist')), parts along dimension 0, may hold values from 16 to 128, as said below
- star_pixel: int32 [32, 16, 128], P(('chain', 'ang', 'dist')), parts along dimension 0, may hold values from 0 to 65535
- star_bin: int32 [32, 16, 128], P(('chain', 'ang', 'dist')), parts along dimension 0, may hold values from 0 to 127
- star_obs: float32 [32, 16, 8, 128], P(('chain', 'ang', 'dist')), parts along dimension 0, may hold values from 0 to 8
- star_isig: float32 [32, 16, 8, 128], P(('chain', 'ang', 'dist')), parts along dimension 0, may hold values from 0.5 to 5
Outputs:
- gradient: float32 [1024, 512, 512], P(('chain', 'dist'), 'ang'), parts along dimension 0
The draws below stay inside these ranges and needn't reach their ends.
There are 2 independent parts, one for each index of `chain`. The reference program is written for one: setup_inputs(seed, part) draws one part's arguments, and reference() takes and returns one part's arrays. A program takes and returns all parts, laid end to end along the dimension named above; an argument that names none is the same for every part. Nothing has to cross between parts.
Inputs may be any that keep to these rules, and one draw needn't show every extreme that they name: The first star_counts[s, d] slots of a bucket hold stars, the rest are empty. In every draw one voxel owner has all 128 slots live from every star owner. `star_pixel`: Row-major index (column offset, row) within the 512 // 4 columns and 512 rows of the voxel owner. `star_bin`: offset within the voxel owner's 128 bins.
All inputs are finite; a program needn't handle non-finite values.
Results may differ from the reference program's by a relative error of at most 0.0062.
Values may be sent and summed in bfloat16 or wider, within the bound.
A program may use at most 320 MiB of HBM per device.

```python
import math
import jax
import jax.numpy as jnp
from jax import lax

NA = 512
NB = 512
K = 512
BANDS = 8
CAP = 128
OWNERS = 16
BIN_DEV = 128
BLOCK_PIX = 65536
N_ANG = 4
N_DIST = 4


def draw_star_counts(key, part):
    key_upper = jax.random.fold_in(key, 101)
    key_chosen = jax.random.fold_in(key, 202)
    key_counts = jax.random.fold_in(key, 303)
    owner = jnp.arange(OWNERS, dtype=jnp.int32)
    upper = jax.random.randint(key_upper, (OWNERS,), CAP // 4, CAP + 1)
    chosen = jax.random.randint(key_chosen, (), 0, OWNERS)
    upper = jnp.where(owner == chosen, CAP, upper)
    lower = upper // 2
    counts = jax.random.randint(key_counts, (OWNERS, OWNERS), lower[None, :], upper[None, :] + 1)
    counts = jnp.where(owner[None, :] == chosen, CAP, counts)
    return counts.astype(jnp.int32)


def with_ends(values, rng, least, high):
    longest = values.shape.index(max(values.shape))
    spots = []
    for shift in (0, 1):
        where = [jax.random.randint(jax.random.fold_in(rng, axis), (), 0, length) for axis, length in enumerate(values.shape)]
        where[longest] = (where[longest] + shift) % values.shape[longest]
        spots.append(tuple(where))
    return values.at[spots[0]].set(least).at[spots[1]].set(high)


def levels(stream_key, extent, cuts, least, largest):
    def one(position, shards_of):
        draws = jax.random.uniform(jax.random.fold_in(jax.random.fold_in(stream_key, 6), position), (shards_of,), jnp.float32, least / len(cuts), largest / len(cuts))
        return jnp.repeat(jnp.exp(draws), extent[position] // shards_of).reshape((-1,) + (1,) * (len(extent) - position - 1))

    factor_of = one(*cuts[0])
    for cut in cuts[1:]:
        factor_of = factor_of * one(*cut)
    return factor_of


def gaussian(key, extent, deviation, reach, cuts=(), held_as=jnp.bfloat16):
    array = jax.random.normal(key, extent, jnp.float32) * deviation
    if len(cuts) > 0:
        array = levels(key, extent, cuts, -0.22, 0.18) * array
    return jnp.clip(array, min=-reach, max=reach).astype(held_as)


def setup_inputs(seed: int = 0, part: int = 0) -> dict:
    streams_of = jax.random.split(jax.random.key(seed), 11)
    part_keys = jax.random.split(jax.random.fold_in(streams_of[10], part), 11)
    latent = gaussian(part_keys[0], (K, NA, NB), 1.0, 6.0, ((0, 4), (1, 4)), jnp.float32)
    row_factor = gaussian(streams_of[1], (NA, NA), NA ** -0.5, 0.25)
    col_factor = gaussian(streams_of[2], (NB, NB), NB ** -0.5, 0.25)
    log_mean = jnp.clip(-6.0 + 2.0 * jax.random.uniform(part_keys[3], (K,), jnp.float32) ** levels(part_keys[3], (K,), ((0, 4),), -0.2, 0.2), -6.0, -4.0)
    band_ratio = jnp.clip(jnp.exp(jax.random.uniform(streams_of[4], (BANDS,), jnp.float32, math.log(0.2), math.log(2.0))), 0.2, 2.0)
    star_counts = draw_star_counts(jax.random.fold_in(jax.random.fold_in(streams_of[10], part), 71), part)
    star_pixel = with_ends(jax.random.randint(part_keys[6], (OWNERS, OWNERS, CAP), 0, BLOCK_PIX), jax.random.fold_in(part_keys[6], 1), 0, BLOCK_PIX - 1).astype(jnp.int32)
    star_bin = with_ends(jax.random.randint(part_keys[7], (OWNERS, OWNERS, CAP), 0, BIN_DEV), jax.random.fold_in(part_keys[7], 1), 0, BIN_DEV - 1).astype(jnp.int32)
    star_obs = jnp.clip(8.0 * jax.random.uniform(part_keys[8], (OWNERS, OWNERS, BANDS, CAP), jnp.float32) ** levels(part_keys[8], (OWNERS, OWNERS, BANDS, CAP), ((0, 16),), -0.2, 0.2), 0.0, 8.0)
    star_isig = jnp.clip(jnp.exp(math.log(5.0) - 2.3025851 * jax.random.uniform(part_keys[9], (OWNERS, OWNERS, BANDS, CAP), jnp.float32) ** levels(part_keys[9], (OWNERS, OWNERS, BANDS, CAP), ((0, 16),), -0.2, 0.2)), 0.5, 5.0)
    return dict(latent=latent, row_factor=row_factor, col_factor=col_factor, log_mean=log_mean, band_ratio=band_ratio, star_counts=star_counts, star_pixel=star_pixel, star_bin=star_bin, star_obs=star_obs, star_isig=star_isig)


def reference(latent, row_factor, col_factor, log_mean, band_ratio, star_counts, star_pixel, star_bin, star_obs, star_isig):
    bin_count, grid_rows, grid_cols = latent.shape
    latent_bf = latent.astype(jnp.bfloat16)
    inner = jnp.dot(latent_bf.reshape(-1, grid_cols), col_factor.T, preferred_element_type=jnp.float32).astype(jnp.bfloat16)
    inner = jnp.transpose(inner.reshape(bin_count, grid_rows, grid_cols), (0, 2, 1)).reshape(-1, grid_rows)
    field = jnp.dot(inner, row_factor.T, preferred_element_type=jnp.float32).reshape(bin_count, grid_cols, grid_rows)
    density = jnp.exp(log_mean[:, None, None] + field)
    extinction = jnp.cumsum(density, axis=0)
    capacity = star_pixel.shape[-1]
    live = jnp.arange(capacity, dtype=jnp.int32)[None, None, :] < star_counts[:, :, None]
    weight = jnp.where(live[:, :, None, :], star_isig, jnp.zeros_like(star_isig))
    owner = jnp.arange(OWNERS, dtype=jnp.int32)[None, :, None]
    col_index = (owner // N_DIST) * (grid_cols // N_ANG) + star_pixel // grid_rows
    row_index = star_pixel % grid_rows
    bin_index = (owner % N_DIST) * (bin_count // N_DIST) + star_bin
    flat_index = ((bin_index * grid_cols + col_index) * grid_rows + row_index).astype(jnp.int32)
    predicted = extinction.reshape(-1)[flat_index]
    ratio = band_ratio[None, None, :, None]
    resid = (ratio * predicted[:, :, None, :] - star_obs) * weight
    coeff = jnp.sum(ratio * weight * resid, axis=2)
    grad_ext = jnp.zeros((bin_count * grid_cols * grid_rows,), jnp.float32)
    grad_ext = grad_ext.at[flat_index.reshape(-1)].add(coeff.reshape(-1)).reshape(bin_count, grid_cols, grid_rows)
    grad_density = lax.cumsum(grad_ext, axis=0, reverse=True)
    grad_field = (grad_density * density).astype(jnp.bfloat16)
    back = jnp.dot(grad_field.reshape(-1, grid_rows), row_factor, preferred_element_type=jnp.float32).astype(jnp.bfloat16)
    back = jnp.transpose(back.reshape(bin_count, grid_cols, grid_rows), (0, 2, 1)).reshape(-1, grid_cols)
    adjoint = jnp.dot(back, col_factor, preferred_element_type=jnp.float32).reshape(bin_count, grid_rows, grid_cols)
    return latent + adjoint
```

```python
import functools

import jax
import jax.numpy as jnp
from jax import lax
from jax.experimental import pallas as pl
from jax.experimental.pallas import tpu as pltpu
from jax.sharding import PartitionSpec as P

LANES = 128
CHUNKS = 4
STEP = 8
VMEM = 48 << 20


def nearer_sum(totals):
    every = lax.all_gather(totals[None], "dist", axis=0, tiled=True)
    position = jnp.arange(every.shape[0], dtype=jnp.int32)
    keep = position < lax.axis_index("dist")
    return jnp.sum(jnp.where(keep[:, None, None], every, 0.0), axis=0)


def farther_sum(totals):
    every = lax.all_gather(totals[None], "dist", axis=0, tiled=True)
    position = jnp.arange(every.shape[0], dtype=jnp.int32)
    keep = position > lax.axis_index("dist")
    return jnp.sum(jnp.where(keep[:, None, None], every, 0.0), axis=0)


def general(
    latent,
    row_factor,
    col_factor,
    log_mean,
    band_ratio,
    star_counts,
    star_pixel,
    star_bin,
    star_obs,
    star_isig,
):
    latent_bf = latent.astype(jnp.bfloat16)
    inner = jnp.einsum(
        "kab,cb->kca", latent_bf, col_factor, preferred_element_type=jnp.float32
    ).astype(jnp.bfloat16)
    field = jnp.einsum(
        "kca,ea->kce",
        lax.all_to_all(inner, "ang", split_axis=1, concat_axis=2, tiled=True),
        row_factor,
        preferred_element_type=jnp.float32,
    )
    density = jnp.exp(log_mean[:, None, None] + field)
    running = lax.cumsum(density, axis=0)
    extinction = running + nearer_sum(running[-1])[None]
    capacity = star_pixel.shape[-1]
    live = jnp.arange(capacity, dtype=jnp.int32)[None, None, :] < star_counts[:, :, None]
    weight = jnp.where(live[:, :, None, :], star_isig, 0.0)
    depth = star_obs.shape[2]
    pixel_in, bin_in = (
        lax.all_to_all(star_pixel, ("ang", "dist"), split_axis=1, concat_axis=0, tiled=True),
        lax.all_to_all(star_bin, ("ang", "dist"), split_axis=1, concat_axis=0, tiled=True),
    )
    first_in, second_in = (
        lax.all_to_all(star_obs, ("ang", "dist"), split_axis=1, concat_axis=0, tiled=True),
        lax.all_to_all(weight, ("ang", "dist"), split_axis=1, concat_axis=0, tiled=True),
    )
    pixel_in = pixel_in.reshape(-1, capacity)
    bin_in = bin_in.reshape(-1, capacity)
    first_in = first_in.reshape(-1, depth, capacity)
    second_in = second_in.reshape(-1, depth, capacity)
    block_pixels = extinction.shape[1] * extinction.shape[2]
    flat_index = bin_in * block_pixels + pixel_in
    predicted = extinction.reshape(-1)[flat_index]
    ratio = band_ratio[None, :, None]
    resid = (ratio * predicted[:, None, :] - first_in) * second_in
    coeff = jnp.sum(ratio * second_in * resid, axis=1)
    grad_ext = jnp.zeros((extinction.size,), jnp.float32)
    grad_ext = grad_ext.at[flat_index.reshape(-1)].add(coeff.reshape(-1)).reshape(extinction.shape)
    back_running = lax.cumsum(grad_ext, axis=0, reverse=True)
    grad_density = back_running + farther_sum(back_running[0])[None]
    grad_field = (grad_density * density).astype(jnp.bfloat16)
    back = jnp.einsum(
        "kce,ea->kca", grad_field, row_factor, preferred_element_type=jnp.float32
    ).astype(jnp.bfloat16)
    returned = lax.all_to_all(back, "ang", split_axis=2, concat_axis=1, tiled=True)
    adjoint = jnp.einsum("kca,cb->kab", returned, col_factor, preferred_element_type=jnp.float32)
    return latent + adjoint


def dot_nt(x, y):
    return lax.dot_general(x, y, (((1,), (1,)), ((), ())), preferred_element_type=jnp.float32)


def split_store(product, out_refs):
    for block, out_ref in enumerate(out_refs):
        for k in range(out_ref.shape[0]):
            out_ref[k] = product[
                block * LANES : (block + 1) * LANES, k * LANES : (k + 1) * LANES
            ].astype(out_ref.dtype)


def joined(refs):
    return jnp.concatenate([ref[...].reshape(-1, LANES) for ref in refs], axis=1)


def column_kernel(latent_ref, col_ref, *out_refs):
    block = latent_ref[...].astype(jnp.bfloat16).reshape(-1, latent_ref.shape[2])
    split_store(dot_nt(col_ref[...], block), out_refs)


def density_kernel(parts, chained, mean_ref, row_ref, start_ref, *refs):
    in_refs = refs[:parts]
    running_ref, density_ref, total_ref = refs[parts + (2 if chained else 0) :]
    step = pl.program_id(0)

    @pl.when(step == 0)
    def _():
        total_ref[...] = start_ref[...]

    field = dot_nt(joined(in_refs), row_ref[...])
    for slab in range(field.shape[1] // LANES):
        rows = slice(slab * LANES, (slab + 1) * LANES)
        total = total_ref[rows]
        for k in range(STEP):
            density = jnp.exp(mean_ref[step * STEP + k] + field[k * LANES : (k + 1) * LANES, rows])
            total = total + density
            running_ref[k, rows] = total
            density_ref[k, rows] = density.astype(density_ref.dtype)
        total_ref[rows] = total


def adjoint_kernel(row_ref, start_ref, grad_ref, density_ref, *refs):
    *out_refs, total_ref, field_ref = refs

    @pl.when(pl.program_id(0) == 0)
    def _():
        total_ref[...] = start_ref[...]

    for slab in range(total_ref.shape[0] // LANES):
        rows = slice(slab * LANES, (slab + 1) * LANES)
        total = total_ref[rows]
        for k in reversed(range(STEP)):
            total = total + grad_ref[k, rows]
            field_ref[k * LANES : (k + 1) * LANES, rows] = (
                total * density_ref[k, rows].astype(jnp.float32)
            ).astype(jnp.bfloat16)
        total_ref[rows] = total
    split_store(dot_nt(row_ref[...], field_ref[...]), out_refs)


def output_kernel(parts, latent_ref, col_ref, *refs):
    in_refs, out_ref = refs[:parts], refs[-1]
    adjoint = jnp.dot(joined(in_refs), col_ref[...], preferred_element_type=jnp.float32)
    out_ref[...] = latent_ref[...] + adjoint.reshape(out_ref.shape)


def call(kernel, cost, **kwargs):
    return pl.pallas_call(
        kernel,
        compiler_params=pltpu.CompilerParams(vmem_limit_bytes=VMEM),
        cost_estimate=pl.CostEstimate(flops=cost[0], bytes_accessed=cost[1], transcendentals=0),
        **kwargs,
    )


def exchange(parts):
    count = len(parts)
    return [parts[0]] + [
        lax.ppermute(parts[b], "ang", [(i, i ^ b) for i in range(count)]) for b in range(1, count)
    ]


def masked_sum(totals, nearer):
    every = lax.all_gather(totals[None], "dist", axis=0, tiled=True)
    position = jnp.arange(every.shape[0], dtype=jnp.int32)
    me = lax.axis_index("dist")
    keep = position < me if nearer else position > me
    return jnp.sum(jnp.where(keep[:, None, None], every, 0.0), axis=0)


def fused(
    parts,
    latent,
    row_factor,
    col_factor,
    log_mean,
    band_ratio,
    star_counts,
    star_pixel,
    star_bin,
    star_obs,
    star_isig,
):
    bins, rows, cols = latent.shape
    all_rows = rows * parts
    slabs = all_rows // LANES
    pixel_rows = slabs * LANES
    me = lax.axis_index("ang")
    order = me ^ jnp.arange(parts, dtype=jnp.int32)
    col_order = col_factor.reshape(parts, LANES, cols)[order].reshape(cols, cols)
    row_order = (
        row_factor.reshape(all_rows, parts, LANES)[:, order].reshape(all_rows, all_rows)
    )
    row_turned = row_order.T

    capacity = star_pixel.shape[-1]
    live = jnp.arange(capacity, dtype=jnp.int32)[None, None, :] < star_counts[:, :, None]
    ratio = band_ratio[None, None, :, None]
    pull = ratio * jnp.where(live[:, :, None, :], star_isig, 0.0) ** 2
    slope = jnp.sum(pull * ratio, axis=2)
    offset = jnp.sum(pull * star_obs, axis=2)
    star_row = star_pixel % all_rows
    pixel = ((star_row // LANES) * LANES + star_pixel // all_rows) * LANES + star_row % LANES
    block_pixels = pixel_rows * LANES
    voxel = star_bin * block_pixels + pixel
    packed = jnp.stack([voxel.astype(jnp.float32), slope, offset], axis=2)
    packed = lax.all_to_all(packed, ("ang", "dist"), split_axis=1, concat_axis=0, tiled=True)
    packed = packed.reshape(-1, 3, capacity)
    voxel = packed[:, 0].astype(jnp.int32).reshape(-1)
    slope, offset = packed[:, 1].reshape(-1), packed[:, 2].reshape(-1)
    pixel = voxel % block_pixels
    at_row = (pixel[:, None] // LANES == jnp.arange(pixel_rows)[None]).astype(jnp.float32)
    at_lane = (pixel[:, None] % LANES == jnp.arange(LANES)[None]).astype(jnp.float32)

    chunk = bins // CHUNKS
    steps = chunk // STEP
    flops = 2 * chunk * rows * cols * all_rows
    whole = lambda shape: pl.BlockSpec(shape, lambda i: (0,) * len(shape))
    piece = pl.BlockSpec((STEP, LANES, LANES), lambda i: (i, 0, 0))
    pieces = [jax.ShapeDtypeStruct((chunk, LANES, LANES), jnp.bfloat16)] * parts
    anywhere = pl.BlockSpec(memory_space=pl.ANY)

    def placed(shape, c, back=False):
        if back:
            return pl.BlockSpec(shape, lambda i: (c * steps + steps - 1 - i, 0, 0))
        return pl.BlockSpec(shape, lambda i: (c * steps + i, 0, 0))

    latent_block = (STEP, rows, cols)
    pixel_block = (STEP, pixel_rows, LANES)

    arrived = []
    for c in range(CHUNKS):
        sent = call(
            column_kernel,
            (flops, chunk * rows * cols * 6),
            grid=(steps,),
            in_specs=[placed(latent_block, c), whole((cols, cols))],
            out_specs=[piece] * parts,
            out_shape=pieces,
        )(latent, col_order)
        arrived.append(exchange(sent))

    kept = []
    total = jnp.zeros((pixel_rows, LANES), jnp.float32)
    for c in range(CHUNKS):
        *kept, total = call(
            functools.partial(density_kernel, parts, c > 0),
            (flops, chunk * rows * cols * 8),
            grid=(steps,),
            in_specs=[
                pl.BlockSpec(memory_space=pltpu.SMEM),
                whole((all_rows, all_rows)),
                whole((pixel_rows, LANES)),
            ]
            + [piece] * parts
            + [anywhere] * len(kept),
            out_specs=[
                placed(pixel_block, c),
                placed(pixel_block, c),
                whole((pixel_rows, LANES)),
            ],
            out_shape=[
                jax.ShapeDtypeStruct((bins, pixel_rows, LANES), jnp.float32),
                jax.ShapeDtypeStruct((bins, pixel_rows, LANES), jnp.bfloat16),
                jax.ShapeDtypeStruct((pixel_rows, LANES), jnp.float32),
            ],
            input_output_aliases={3 + parts + n: n for n in range(len(kept))},
        )(log_mean[c * chunk : (c + 1) * chunk], row_order, total, *arrived[c], *kept)
    running, density = kept

    exact = lax.Precision.HIGHEST
    nearer = masked_sum(total, True)
    before = jnp.sum(jnp.dot(at_row, nearer, precision=exact) * at_lane, axis=1)
    predicted = running.reshape(-1)[voxel] + before
    coeff = slope * predicted - offset
    grad_ext = jnp.zeros((bins * block_pixels,), jnp.float32).at[voxel].add(coeff)
    grad_ext = grad_ext.reshape(bins, pixel_rows, LANES)
    own = lax.dot_general(
        at_row, at_lane * coeff[:, None], (((0,), (0,)), ((), ())), precision=exact
    )
    total = masked_sum(own, False)

    arrived = [None] * CHUNKS
    for c in reversed(range(CHUNKS)):
        *sent, total = call(
            adjoint_kernel,
            (flops, chunk * rows * cols * 8),
            grid=(steps,),
            in_specs=[
                whole((all_rows, all_rows)),
                whole((pixel_rows, LANES)),
                placed(pixel_block, c, True),
                placed(pixel_block, c, True),
            ],
            out_specs=[pl.BlockSpec((STEP, LANES, LANES), lambda i: (steps - 1 - i, 0, 0))]
            * parts
            + [whole((pixel_rows, LANES))],
            out_shape=pieces + [jax.ShapeDtypeStruct((pixel_rows, LANES), jnp.float32)],
            scratch_shapes=[pltpu.VMEM((STEP * LANES, all_rows), jnp.bfloat16)],
        )(row_turned, total, grad_ext, density)
        arrived[c] = exchange(sent)

    out = []
    for c in reversed(range(CHUNKS)):
        out = call(
            functools.partial(output_kernel, parts),
            (flops, chunk * rows * cols * 10),
            grid=(steps,),
            in_specs=[placed(latent_block, c), whole((cols, cols))]
            + [piece] * parts
            + [anywhere] * len(out),
            out_specs=[placed(latent_block, c)],
            out_shape=[jax.ShapeDtypeStruct((bins, rows, cols), jnp.float32)],
            input_output_aliases={2 + parts + n: n for n in range(len(out))},
        )(latent, col_order, *arrived[c], *out)
    return out[0]


def per_device(parts, latent, *others):
    bins, rows, cols = latent.shape
    tiles = rows == LANES and cols == parts * LANES and bins % (CHUNKS * STEP) == 0
    if tiles and parts & (parts - 1) == 0 and bins * rows * cols <= 1 << 24:
        return fused(parts, latent, *others)
    return general(latent, *others)


def solution(mesh):
    in_specs = (
        P(("chain", "dist"), "ang", None),
        P(),
        P(),
        P(("chain", "dist")),
        P(),
        P(("chain", "ang", "dist"), None),
        P(("chain", "ang", "dist"), None, None),
        P(("chain", "ang", "dist"), None, None),
        P(("chain", "ang", "dist"), None, None, None),
        P(("chain", "ang", "dist"), None, None, None),
    )
    out_specs = P(("chain", "dist"), "ang", None)
    return jax.shard_map(
        functools.partial(per_device, mesh.shape["ang"]), mesh=mesh, in_specs=in_specs, out_specs=out_specs, check_vma=False
    )
```

```python
import functools

import jax
import jax.numpy as jnp
from jax import lax
from jax.experimental import pallas as pl
from jax.experimental.pallas import tpu as pltpu
from jax.sharding import PartitionSpec as P

LANES = 128
CHUNKS = 4
STEP = 8
UNROLL = 16
VMEM = 48 << 20


def nearer_sum(totals):
    every = lax.all_gather(totals[None], "dist", axis=0, tiled=True)
    position = jnp.arange(every.shape[0], dtype=jnp.int32)
    keep = position < lax.axis_index("dist")
    return jnp.sum(jnp.where(keep[:, None, None], every, 0.0), axis=0)


def farther_sum(totals):
    every = lax.all_gather(totals[None], "dist", axis=0, tiled=True)
    position = jnp.arange(every.shape[0], dtype=jnp.int32)
    keep = position > lax.axis_index("dist")
    return jnp.sum(jnp.where(keep[:, None, None], every, 0.0), axis=0)


def general(
    latent,
    row_factor,
    col_factor,
    log_mean,
    band_ratio,
    star_counts,
    star_pixel,
    star_bin,
    star_obs,
    star_isig,
):
    latent_bf = latent.astype(jnp.bfloat16)
    inner = jnp.einsum(
        "kab,cb->kca", latent_bf, col_factor, preferred_element_type=jnp.float32
    ).astype(jnp.bfloat16)
    field = jnp.einsum(
        "kca,ea->kce",
        lax.all_to_all(inner, "ang", split_axis=1, concat_axis=2, tiled=True),
        row_factor,
        preferred_element_type=jnp.float32,
    )
    density = jnp.exp(log_mean[:, None, None] + field)
    running = lax.cumsum(density, axis=0)
    extinction = running + nearer_sum(running[-1])[None]
    capacity = star_pixel.shape[-1]
    live = jnp.arange(capacity, dtype=jnp.int32)[None, None, :] < star_counts[:, :, None]
    weight = jnp.where(live[:, :, None, :], star_isig, 0.0)
    depth = star_obs.shape[2]
    pixel_in, bin_in = (
        lax.all_to_all(star_pixel, ("ang", "dist"), split_axis=1, concat_axis=0, tiled=True),
        lax.all_to_all(star_bin, ("ang", "dist"), split_axis=1, concat_axis=0, tiled=True),
    )
    first_in, second_in = (
        lax.all_to_all(star_obs, ("ang", "dist"), split_axis=1, concat_axis=0, tiled=True),
        lax.all_to_all(weight, ("ang", "dist"), split_axis=1, concat_axis=0, tiled=True),
    )
    pixel_in = pixel_in.reshape(-1, capacity)
    bin_in = bin_in.reshape(-1, capacity)
    first_in = first_in.reshape(-1, depth, capacity)
    second_in = second_in.reshape(-1, depth, capacity)
    block_pixels = extinction.shape[1] * extinction.shape[2]
    flat_index = bin_in * block_pixels + pixel_in
    predicted = extinction.reshape(-1)[flat_index]
    ratio = band_ratio[None, :, None]
    resid = (ratio * predicted[:, None, :] - first_in) * second_in
    coeff = jnp.sum(ratio * second_in * resid, axis=1)
    grad_ext = jnp.zeros((extinction.size,), jnp.float32)
    grad_ext = grad_ext.at[flat_index.reshape(-1)].add(coeff.reshape(-1)).reshape(extinction.shape)
    back_running = lax.cumsum(grad_ext, axis=0, reverse=True)
    grad_density = back_running + farther_sum(back_running[0])[None]
    grad_field = (grad_density * density).astype(jnp.bfloat16)
    back = jnp.einsum(
        "kce,ea->kca", grad_field, row_factor, preferred_element_type=jnp.float32
    ).astype(jnp.bfloat16)
    returned = lax.all_to_all(back, "ang", split_axis=2, concat_axis=1, tiled=True)
    adjoint = jnp.einsum("kca,cb->kab", returned, col_factor, preferred_element_type=jnp.float32)
    return latent + adjoint


def dot_nt(x, y):
    return lax.dot_general(x, y, (((1,), (1,)), ((), ())), preferred_element_type=jnp.float32)


def split_store(product, out_refs):
    for block, out_ref in enumerate(out_refs):
        for k in range(out_ref.shape[0]):
            out_ref[k] = product[
                block * LANES : (block + 1) * LANES, k * LANES : (k + 1) * LANES
            ].astype(out_ref.dtype)


def joined(refs):
    return jnp.concatenate([ref[...].reshape(-1, LANES) for ref in refs], axis=1)


def column_kernel(latent_ref, col_ref, *out_refs):
    block = latent_ref[...].astype(jnp.bfloat16).reshape(-1, latent_ref.shape[2])
    split_store(dot_nt(col_ref[...], block), out_refs)


def density_kernel(parts, chained, mean_ref, voxel_row_ref, row_ref, start_ref, *refs):
    in_refs = refs[:parts]
    density_ref, total_ref, picked_ref, table_ref = refs[parts + (1 if chained else 0) :]
    step = pl.program_id(0)

    @pl.when(step == 0)
    def _():
        total_ref[...] = start_ref[...]

    field = dot_nt(joined(in_refs), row_ref[...])
    for slab in range(field.shape[1] // LANES):
        rows = slice(slab * LANES, (slab + 1) * LANES)
        total = total_ref[rows]
        for k in range(STEP):
            density = jnp.exp(mean_ref[step * STEP + k] + field[k * LANES : (k + 1) * LANES, rows])
            total = total + density
            place = (step * STEP + k) * field.shape[1] + slab * LANES
            table_ref[pl.ds(pl.multiple_of(place, LANES), LANES), :] = total
            density_ref[k, rows] = density.astype(density_ref.dtype)
        total_ref[rows] = total

    @pl.when(step == pl.num_programs(0) - 1)
    def _():
        def pick(i, carry):
            first = i * UNROLL
            found = [
                table_ref[pl.ds(voxel_row_ref[first + j], 1), :] for j in range(UNROLL)
            ]
            for j in range(UNROLL):
                picked_ref[pl.ds(first + j, 1), :] = found[j]
            return carry

        lax.fori_loop(0, picked_ref.shape[0] // UNROLL, pick, 0)


def adjoint_kernel(voxel_row_ref, row_ref, start_ref, value_ref, density_ref, *refs):
    *out_refs, total_ref, field_ref, table_ref = refs
    step = pl.program_id(0)
    block = pl.num_programs(0) - 1 - step

    @pl.when(step == 0)
    def _():
        total_ref[...] = start_ref[...]

        def clear(i, carry):
            place = pl.multiple_of(i * LANES, LANES)
            table_ref[pl.ds(place, LANES), :] = jnp.zeros((LANES, LANES), jnp.float32)
            return carry

        lax.fori_loop(0, table_ref.shape[0] // LANES, clear, 0)

        def add(i, carry):
            for j in range(UNROLL):
                place = pl.ds(voxel_row_ref[i * UNROLL + j], 1)
                table_ref[place, :] = table_ref[place, :] + value_ref[pl.ds(i * UNROLL + j, 1), :]
            return carry

        lax.fori_loop(0, value_ref.shape[0] // UNROLL, add, 0)

    for slab in range(total_ref.shape[0] // LANES):
        rows = slice(slab * LANES, (slab + 1) * LANES)
        total = total_ref[rows]
        for k in reversed(range(STEP)):
            place = (block * STEP + k) * total_ref.shape[0] + slab * LANES
            total = total + table_ref[pl.ds(pl.multiple_of(place, LANES), LANES), :]
            field_ref[k * LANES : (k + 1) * LANES, rows] = (
                total * density_ref[k, rows].astype(jnp.float32)
            ).astype(jnp.bfloat16)
        total_ref[rows] = total
    split_store(dot_nt(row_ref[...], field_ref[...]), out_refs)


def output_kernel(parts, latent_ref, col_ref, *refs):
    in_refs, out_ref = refs[:parts], refs[-1]
    adjoint = jnp.dot(joined(in_refs), col_ref[...], preferred_element_type=jnp.float32)
    out_ref[...] = latent_ref[...] + adjoint.reshape(out_ref.shape)


def call(kernel, cost, **kwargs):
    return pl.pallas_call(
        kernel,
        compiler_params=pltpu.CompilerParams(vmem_limit_bytes=VMEM),
        cost_estimate=pl.CostEstimate(flops=cost[0] // 16, bytes_accessed=cost[1] // 16, transcendentals=0),
        **kwargs,
    )


def exchange(parts):
    count = len(parts)
    return [parts[0]] + [
        lax.ppermute(parts[b], "ang", [(i, i ^ b) for i in range(count)]) for b in range(1, count)
    ]


def masked_sum(totals, nearer):
    every = lax.all_gather(totals[None], "dist", axis=0, tiled=True)
    position = jnp.arange(every.shape[0], dtype=jnp.int32)
    me = lax.axis_index("dist")
    keep = position < me if nearer else position > me
    return jnp.sum(jnp.where(keep[:, None, None], every, 0.0), axis=0)


def fused(
    parts,
    latent,
    row_factor,
    col_factor,
    log_mean,
    band_ratio,
    star_counts,
    star_pixel,
    star_bin,
    star_obs,
    star_isig,
):
    bins, rows, cols = latent.shape
    all_rows = rows * parts
    slabs = all_rows // LANES
    pixel_rows = slabs * LANES
    me = lax.axis_index("ang")
    order = me ^ jnp.arange(parts, dtype=jnp.int32)
    col_order = col_factor.reshape(parts, LANES, cols)[order].reshape(cols, cols)
    row_order = (
        row_factor.reshape(all_rows, parts, LANES)[:, order].reshape(all_rows, all_rows)
    )
    row_turned = row_order.T

    capacity = star_pixel.shape[-1]
    live = jnp.arange(capacity, dtype=jnp.int32)[None, None, :] < star_counts[:, :, None]
    ratio = band_ratio[None, None, :, None]
    pull = ratio * jnp.where(live[:, :, None, :], star_isig, 0.0) ** 2
    slope = jnp.sum(pull * ratio, axis=2)
    offset = jnp.sum(pull * star_obs, axis=2)
    star_row = star_pixel % all_rows
    pixel = ((star_row // LANES) * LANES + star_pixel // all_rows) * LANES + star_row % LANES
    block_pixels = pixel_rows * LANES
    voxel = star_bin * block_pixels + pixel
    packed = jnp.stack([voxel.astype(jnp.float32), slope, offset], axis=2)
    packed = lax.all_to_all(packed, ("ang", "dist"), split_axis=1, concat_axis=0, tiled=True)
    packed = packed.reshape(-1, 3, capacity)
    voxel = packed[:, 0].astype(jnp.int32).reshape(-1)
    slope, offset = packed[:, 1].reshape(-1), packed[:, 2].reshape(-1)
    pixel = voxel % block_pixels
    at_row = (pixel[:, None] // LANES == jnp.arange(pixel_rows)[None]).astype(jnp.float32)
    at_lane = (pixel[:, None] % LANES == jnp.arange(LANES)[None]).astype(jnp.float32)

    chunk = bins // CHUNKS
    steps = chunk // STEP
    flops = 2 * chunk * rows * cols * all_rows
    whole = lambda shape: pl.BlockSpec(shape, lambda i: (0,) * len(shape))
    piece = pl.BlockSpec((STEP, LANES, LANES), lambda i: (i, 0, 0))
    pieces = [jax.ShapeDtypeStruct((chunk, LANES, LANES), jnp.bfloat16)] * parts
    anywhere = pl.BlockSpec(memory_space=pl.ANY)

    def placed(shape, c, back=False):
        if back:
            return pl.BlockSpec(shape, lambda i: (c * steps + steps - 1 - i, 0, 0))
        return pl.BlockSpec(shape, lambda i: (c * steps + i, 0, 0))

    latent_block = (STEP, rows, cols)
    pixel_block = (STEP, pixel_rows, LANES)

    arrived = []
    for c in range(CHUNKS):
        sent = call(
            column_kernel,
            (flops, chunk * rows * cols * 6),
            grid=(steps,),
            in_specs=[placed(latent_block, c), whole((cols, cols))],
            out_specs=[piece] * parts,
            out_shape=pieces,
        )(latent, col_order)
        arrived.append(exchange(sent))

    table_rows = chunk * pixel_rows
    stars = voxel.shape[0]
    voxel_row = [
        jnp.clip(voxel // LANES - c * table_rows, 0, table_rows - 1) for c in range(CHUNKS)
    ]
    inside = [(voxel // (table_rows * LANES) == c)[:, None] for c in range(CHUNKS)]
    scalars = pl.BlockSpec(memory_space=pltpu.SMEM)
    table = pltpu.VMEM((table_rows, LANES), jnp.float32)

    kept = []
    total = jnp.zeros((pixel_rows, LANES), jnp.float32)
    found = jnp.zeros((stars, LANES), jnp.float32)
    for c in range(CHUNKS):
        *kept, total, picked = call(
            functools.partial(density_kernel, parts, c > 0),
            (flops, chunk * rows * cols * 4),
            grid=(steps,),
            in_specs=[scalars, scalars, whole((all_rows, all_rows)), whole((pixel_rows, LANES))]
            + [piece] * parts
            + [anywhere] * len(kept),
            out_specs=[
                placed(pixel_block, c),
                whole((pixel_rows, LANES)),
                whole((stars, LANES)),
            ],
            out_shape=[
                jax.ShapeDtypeStruct((bins, pixel_rows, LANES), jnp.bfloat16),
                jax.ShapeDtypeStruct((pixel_rows, LANES), jnp.float32),
                jax.ShapeDtypeStruct((stars, LANES), jnp.float32),
            ],
            scratch_shapes=[table],
            input_output_aliases={4 + parts: 0} if c > 0 else {},
        )(log_mean[c * chunk : (c + 1) * chunk], voxel_row[c], row_order, total, *arrived[c], *kept)
        found = jnp.where(inside[c], picked, found)
    density = kept[0]

    exact = lax.Precision.HIGHEST
    nearer = masked_sum(total, True)
    before = jnp.dot(at_row, nearer, precision=exact)
    predicted = jnp.sum((found + before) * at_lane, axis=1)
    coeff = slope * predicted - offset
    values = at_lane * coeff[:, None]
    own = lax.dot_general(
        at_row, values, (((0,), (0,)), ((), ())), precision=exact
    )
    total = masked_sum(own, False)

    arrived = [None] * CHUNKS
    for c in reversed(range(CHUNKS)):
        *sent, total = call(
            adjoint_kernel,
            (flops, chunk * rows * cols * 4),
            grid=(steps,),
            in_specs=[
                scalars,
                whole((all_rows, all_rows)),
                whole((pixel_rows, LANES)),
                whole((stars, LANES)),
                placed(pixel_block, c, True),
            ],
            out_specs=[pl.BlockSpec((STEP, LANES, LANES), lambda i: (steps - 1 - i, 0, 0))]
            * parts
            + [whole((pixel_rows, LANES))],
            out_shape=pieces + [jax.ShapeDtypeStruct((pixel_rows, LANES), jnp.float32)],
            scratch_shapes=[pltpu.VMEM((STEP * LANES, all_rows), jnp.bfloat16), table],
        )(voxel_row[c], row_turned, total, jnp.where(inside[c], values, 0.0), density)
        arrived[c] = exchange(sent)

    out = []
    for c in reversed(range(CHUNKS)):
        out = call(
            functools.partial(output_kernel, parts),
            (flops, chunk * rows * cols * 10),
            grid=(steps,),
            in_specs=[placed(latent_block, c), whole((cols, cols))]
            + [piece] * parts
            + [anywhere] * len(out),
            out_specs=[placed(latent_block, c)],
            out_shape=[jax.ShapeDtypeStruct((bins, rows, cols), jnp.float32)],
            input_output_aliases={2 + parts + n: n for n in range(len(out))},
        )(latent, col_order, *arrived[c], *out)
    return out[0]


def per_device(parts, latent, *others):
    bins, rows, cols = latent.shape
    tiles = rows == LANES and cols == parts * LANES and bins % (CHUNKS * STEP) == 0
    if tiles and parts & (parts - 1) == 0 and bins * rows * cols <= 1 << 24:
        return fused(parts, latent, *others)
    return general(latent, *others)


def solution(mesh):
    in_specs = (
        P(("chain", "dist"), "ang", None),
        P(),
        P(),
        P(("chain", "dist")),
        P(),
        P(("chain", "ang", "dist"), None),
        P(("chain", "ang", "dist"), None, None),
        P(("chain", "ang", "dist"), None, None),
        P(("chain", "ang", "dist"), None, None, None),
        P(("chain", "ang", "dist"), None, None, None),
    )
    out_specs = P(("chain", "dist"), "ang", None)
    return jax.shard_map(
        functools.partial(per_device, mesh.shape["ang"]), mesh=mesh, in_specs=in_specs, out_specs=out_specs, check_vma=False
    )
```

```python
import functools

import jax
import jax.numpy as jnp
from jax import lax
from jax.experimental import pallas as pl
from jax.experimental.pallas import tpu as pltpu
from jax.sharding import PartitionSpec as P

LANES = 128
CHUNKS = 4
STEP = 8
UNROLL = 16
VMEM = 48 << 20


def nearer_sum(totals):
    every = lax.all_gather(totals[None], "dist", axis=0, tiled=True)
    position = jnp.arange(every.shape[0], dtype=jnp.int32)
    keep = position < lax.axis_index("dist")
    return jnp.sum(jnp.where(keep[:, None, None], every, 0.0), axis=0)


def farther_sum(totals):
    every = lax.all_gather(totals[None], "dist", axis=0, tiled=True)
    position = jnp.arange(every.shape[0], dtype=jnp.int32)
    keep = position > lax.axis_index("dist")
    return jnp.sum(jnp.where(keep[:, None, None], every, 0.0), axis=0)


def general(
    latent,
    row_factor,
    col_factor,
    log_mean,
    band_ratio,
    star_counts,
    star_pixel,
    star_bin,
    star_obs,
    star_isig,
):
    latent_bf = latent.astype(jnp.bfloat16)
    inner = jnp.einsum(
        "kab,cb->kca", latent_bf, col_factor, preferred_element_type=jnp.float32
    ).astype(jnp.bfloat16)
    field = jnp.einsum(
        "kca,ea->kce",
        lax.all_to_all(inner, "ang", split_axis=1, concat_axis=2, tiled=True),
        row_factor,
        preferred_element_type=jnp.float32,
    )
    density = jnp.exp(log_mean[:, None, None] + field)
    running = lax.cumsum(density, axis=0)
    extinction = running + nearer_sum(running[-1])[None]
    capacity = star_pixel.shape[-1]
    live = jnp.arange(capacity, dtype=jnp.int32)[None, None, :] < star_counts[:, :, None]
    weight = jnp.where(live[:, :, None, :], star_isig, 0.0)
    depth = star_obs.shape[2]
    pixel_in, bin_in = (
        lax.all_to_all(star_pixel, ("ang", "dist"), split_axis=1, concat_axis=0, tiled=True),
        lax.all_to_all(star_bin, ("ang", "dist"), split_axis=1, concat_axis=0, tiled=True),
    )
    first_in, second_in = (
        lax.all_to_all(star_obs, ("ang", "dist"), split_axis=1, concat_axis=0, tiled=True),
        lax.all_to_all(weight, ("ang", "dist"), split_axis=1, concat_axis=0, tiled=True),
    )
    pixel_in = pixel_in.reshape(-1, capacity)
    bin_in = bin_in.reshape(-1, capacity)
    first_in = first_in.reshape(-1, depth, capacity)
    second_in = second_in.reshape(-1, depth, capacity)
    block_pixels = extinction.shape[1] * extinction.shape[2]
    flat_index = bin_in * block_pixels + pixel_in
    predicted = extinction.reshape(-1)[flat_index]
    ratio = band_ratio[None, :, None]
    resid = (ratio * predicted[:, None, :] - first_in) * second_in
    coeff = jnp.sum(ratio * second_in * resid, axis=1)
    grad_ext = jnp.zeros((extinction.size,), jnp.float32)
    grad_ext = grad_ext.at[flat_index.reshape(-1)].add(coeff.reshape(-1)).reshape(extinction.shape)
    back_running = lax.cumsum(grad_ext, axis=0, reverse=True)
    grad_density = back_running + farther_sum(back_running[0])[None]
    grad_field = (grad_density * density).astype(jnp.bfloat16)
    back = jnp.einsum(
        "kce,ea->kca", grad_field, row_factor, preferred_element_type=jnp.float32
    ).astype(jnp.bfloat16)
    returned = lax.all_to_all(back, "ang", split_axis=2, concat_axis=1, tiled=True)
    adjoint = jnp.einsum("kca,cb->kab", returned, col_factor, preferred_element_type=jnp.float32)
    return latent + adjoint


def dot_nt(x, y):
    return lax.dot_general(x, y, (((1,), (1,)), ((), ())), preferred_element_type=jnp.float32)


def split_store(product, out_refs):
    for block, out_ref in enumerate(out_refs):
        for k in range(out_ref.shape[0]):
            out_ref[k] = product[
                block * LANES : (block + 1) * LANES, k * LANES : (k + 1) * LANES
            ].astype(out_ref.dtype)


def joined(refs):
    return jnp.concatenate([ref[...].reshape(-1, LANES) for ref in refs], axis=1)


def column_kernel(latent_ref, col_ref, packed_ref, *out_refs):
    block = latent_ref[...].astype(jnp.bfloat16).reshape(-1, latent_ref.shape[2])
    split_store(dot_nt(col_ref[...], block), out_refs)


def density_kernel(parts, chained, mean_ref, voxel_row_ref, row_ref, start_ref, *refs):
    in_refs = refs[:parts]
    density_ref, total_ref, picked_ref, table_ref = refs[parts + (1 if chained else 0) :]
    step = pl.program_id(0)

    @pl.when(step == 0)
    def _():
        total_ref[...] = start_ref[...]

    field = dot_nt(joined(in_refs), row_ref[...])
    for slab in range(field.shape[1] // LANES):
        rows = slice(slab * LANES, (slab + 1) * LANES)
        total = total_ref[rows]
        for k in range(STEP):
            density = jnp.exp(mean_ref[step * STEP + k] + field[k * LANES : (k + 1) * LANES, rows])
            total = total + density
            place = (step * STEP + k) * field.shape[1] + slab * LANES
            table_ref[pl.ds(pl.multiple_of(place, LANES), LANES), :] = total
            density_ref[k, rows] = density.astype(density_ref.dtype)
        total_ref[rows] = total

    @pl.when(step == pl.num_programs(0) - 1)
    def _():
        def pick(i, carry):
            first = i * UNROLL
            found = [
                table_ref[pl.ds(voxel_row_ref[first + j], 1), :] for j in range(UNROLL)
            ]
            for j in range(UNROLL):
                picked_ref[pl.ds(first + j, 1), :] = found[j]
            return carry

        lax.fori_loop(0, picked_ref.shape[0] // UNROLL, pick, 0)


def adjoint_kernel(voxel_row_ref, row_ref, start_ref, value_ref, density_ref, *refs):
    *out_refs, total_ref, field_ref, table_ref = refs
    step = pl.program_id(0)
    block = pl.num_programs(0) - 1 - step

    @pl.when(step == 0)
    def _():
        total_ref[...] = start_ref[...]

        def clear(i, carry):
            place = pl.multiple_of(i * LANES, LANES)
            table_ref[pl.ds(place, LANES), :] = jnp.zeros((LANES, LANES), jnp.float32)
            return carry

        lax.fori_loop(0, table_ref.shape[0] // LANES, clear, 0)

        def add(i, carry):
            for j in range(UNROLL):
                place = pl.ds(voxel_row_ref[i * UNROLL + j], 1)
                table_ref[place, :] = table_ref[place, :] + value_ref[pl.ds(i * UNROLL + j, 1), :]
            return carry

        lax.fori_loop(0, value_ref.shape[0] // UNROLL, add, 0)

    for slab in range(total_ref.shape[0] // LANES):
        rows = slice(slab * LANES, (slab + 1) * LANES)
        total = total_ref[rows]
        for k in reversed(range(STEP)):
            place = (block * STEP + k) * total_ref.shape[0] + slab * LANES
            total = total + table_ref[pl.ds(pl.multiple_of(place, LANES), LANES), :]
            field_ref[k * LANES : (k + 1) * LANES, rows] = (
                total * density_ref[k, rows].astype(jnp.float32)
            ).astype(jnp.bfloat16)
        total_ref[rows] = total
    split_store(dot_nt(row_ref[...], field_ref[...]), out_refs)


def output_kernel(parts, latent_ref, col_ref, *refs):
    in_refs, out_ref = refs[:parts], refs[-1]
    adjoint = jnp.dot(joined(in_refs), col_ref[...], preferred_element_type=jnp.float32)
    out_ref[...] = latent_ref[...] + adjoint.reshape(out_ref.shape)


def call(kernel, cost, **kwargs):
    return pl.pallas_call(
        kernel,
        compiler_params=pltpu.CompilerParams(vmem_limit_bytes=VMEM),
        cost_estimate=pl.CostEstimate(flops=cost[0] // 16, bytes_accessed=cost[1] // 16, transcendentals=0),
        **kwargs,
    )


def exchange(parts):
    count = len(parts)
    return [parts[0]] + [
        lax.ppermute(parts[b], "ang", [(i, i ^ b) for i in range(count)]) for b in range(1, count)
    ]


def other_sum(totals, count, nearer):
    sums, others = totals, jnp.zeros_like(totals)
    shift = 1
    while shift < count:
        pairs = [(i, i + shift) for i in range(count - shift)]
        moved = lax.ppermute(sums, "dist", pairs if nearer else [(j, i) for i, j in pairs])
        sums, others = sums + moved, others + moved
        shift *= 2
    return others


def fused(
    parts,
    dists,
    latent,
    row_factor,
    col_factor,
    log_mean,
    band_ratio,
    star_counts,
    star_pixel,
    star_bin,
    star_obs,
    star_isig,
):
    bins, rows, cols = latent.shape
    all_rows = rows * parts
    slabs = all_rows // LANES
    pixel_rows = slabs * LANES
    me = lax.axis_index("ang")
    order = me ^ jnp.arange(parts, dtype=jnp.int32)
    col_order = col_factor.reshape(parts, LANES, cols)[order].reshape(cols, cols)
    row_order = (
        row_factor.reshape(all_rows, parts, LANES)[:, order].reshape(all_rows, all_rows)
    )
    row_turned = row_order.T

    capacity = star_pixel.shape[-1]
    live = jnp.arange(capacity, dtype=jnp.int32)[None, None, :] < star_counts[:, :, None]
    ratio = band_ratio[None, None, :, None]
    pull = ratio * jnp.where(live[:, :, None, :], star_isig, 0.0) ** 2
    slope = jnp.sum(pull * ratio, axis=2)
    offset = jnp.sum(pull * star_obs, axis=2)
    star_row = star_pixel % all_rows
    pixel = ((star_row // LANES) * LANES + star_pixel // all_rows) * LANES + star_row % LANES
    block_pixels = pixel_rows * LANES
    voxel = star_bin * block_pixels + pixel
    packed = jnp.stack([voxel.astype(jnp.float32), slope, offset], axis=2)
    packed = lax.all_to_all(packed, ("ang", "dist"), split_axis=1, concat_axis=0, tiled=True)
    packed = packed.reshape(-1, 3, capacity)
    voxel = packed[:, 0].astype(jnp.int32).reshape(-1)
    slope, offset = packed[:, 1].reshape(-1), packed[:, 2].reshape(-1)
    pixel = voxel % block_pixels
    at_row = (pixel[:, None] // LANES == jnp.arange(pixel_rows)[None]).astype(jnp.float32)
    at_lane = (pixel[:, None] % LANES == jnp.arange(LANES)[None]).astype(jnp.float32)

    chunk = bins // CHUNKS
    steps = chunk // STEP
    flops = 2 * chunk * rows * cols * all_rows
    whole = lambda shape: pl.BlockSpec(shape, lambda i: (0,) * len(shape))
    piece = pl.BlockSpec((STEP, LANES, LANES), lambda i: (i, 0, 0))
    pieces = [jax.ShapeDtypeStruct((chunk, LANES, LANES), jnp.bfloat16)] * parts
    anywhere = pl.BlockSpec(memory_space=pl.ANY)

    def placed(shape, c, back=False):
        if back:
            return pl.BlockSpec(shape, lambda i: (c * steps + steps - 1 - i, 0, 0))
        return pl.BlockSpec(shape, lambda i: (c * steps + i, 0, 0))

    latent_block = (STEP, rows, cols)
    pixel_block = (STEP, pixel_rows, LANES)

    arrived = []
    for c in range(CHUNKS):
        sent = call(
            column_kernel,
            (flops, chunk * rows * cols * 6),
            grid=(steps,),
            in_specs=[placed(latent_block, c), whole((cols, cols)), anywhere],
            out_specs=[piece] * parts,
            out_shape=pieces,
        )(latent, col_order, packed)
        arrived.append(exchange(sent))

    table_rows = chunk * pixel_rows
    stars = voxel.shape[0]
    voxel_row = [
        jnp.clip(voxel // LANES - c * table_rows, 0, table_rows - 1) for c in range(CHUNKS)
    ]
    inside = [(voxel // (table_rows * LANES) == c)[:, None] for c in range(CHUNKS)]
    scalars = pl.BlockSpec(memory_space=pltpu.SMEM)
    table = pltpu.VMEM((table_rows, LANES), jnp.float32)

    kept = []
    total = jnp.zeros((pixel_rows, LANES), jnp.float32)
    found = jnp.zeros((stars, LANES), jnp.float32)
    for c in range(CHUNKS):
        *kept, total, picked = call(
            functools.partial(density_kernel, parts, c > 0),
            (flops, chunk * rows * cols * 4),
            grid=(steps,),
            in_specs=[scalars, scalars, whole((all_rows, all_rows)), whole((pixel_rows, LANES))]
            + [piece] * parts
            + [anywhere] * len(kept),
            out_specs=[
                placed(pixel_block, c),
                whole((pixel_rows, LANES)),
                whole((stars, LANES)),
            ],
            out_shape=[
                jax.ShapeDtypeStruct((bins, pixel_rows, LANES), jnp.bfloat16),
                jax.ShapeDtypeStruct((pixel_rows, LANES), jnp.float32),
                jax.ShapeDtypeStruct((stars, LANES), jnp.float32),
            ],
            scratch_shapes=[table],
            input_output_aliases={4 + parts: 0} if c > 0 else {},
        )(log_mean[c * chunk : (c + 1) * chunk], voxel_row[c], row_order, total, *arrived[c], *kept)
        found = jnp.where(inside[c], picked, found)
    density = kept[0]

    exact = lax.Precision.HIGHEST
    nearer = other_sum(total, dists, True)
    before = jnp.dot(at_row, nearer, precision=exact)
    predicted = jnp.sum((found + before) * at_lane, axis=1)
    coeff = slope * predicted - offset
    values = at_lane * coeff[:, None]
    own = lax.dot_general(
        at_row, values, (((0,), (0,)), ((), ())), precision=exact
    )
    total = other_sum(own, dists, False)

    arrived = [None] * CHUNKS
    for c in reversed(range(CHUNKS)):
        *sent, total = call(
            adjoint_kernel,
            (flops, chunk * rows * cols * 4),
            grid=(steps,),
            in_specs=[
                scalars,
                whole((all_rows, all_rows)),
                whole((pixel_rows, LANES)),
                whole((stars, LANES)),
                placed(pixel_block, c, True),
            ],
            out_specs=[pl.BlockSpec((STEP, LANES, LANES), lambda i: (steps - 1 - i, 0, 0))]
            * parts
            + [whole((pixel_rows, LANES))],
            out_shape=pieces + [jax.ShapeDtypeStruct((pixel_rows, LANES), jnp.float32)],
            scratch_shapes=[pltpu.VMEM((STEP * LANES, all_rows), jnp.bfloat16), table],
        )(voxel_row[c], row_turned, total, jnp.where(inside[c], values, 0.0), density)
        arrived[c] = exchange(sent)

    out = []
    for c in reversed(range(CHUNKS)):
        out = call(
            functools.partial(output_kernel, parts),
            (flops, chunk * rows * cols * 10),
            grid=(steps,),
            in_specs=[placed(latent_block, c), whole((cols, cols))]
            + [piece] * parts
            + [anywhere] * len(out),
            out_specs=[placed(latent_block, c)],
            out_shape=[jax.ShapeDtypeStruct((bins, rows, cols), jnp.float32)],
            input_output_aliases={2 + parts + n: n for n in range(len(out))},
        )(latent, col_order, *arrived[c], *out)
    return out[0]


def per_device(parts, dists, latent, *others):
    bins, rows, cols = latent.shape
    tiles = rows == LANES and cols == parts * LANES and bins % (CHUNKS * STEP) == 0
    if tiles and parts & (parts - 1) == 0 and bins * rows * cols <= 1 << 24:
        return fused(parts, dists, latent, *others)
    return general(latent, *others)


def solution(mesh):
    in_specs = (
        P(("chain", "dist"), "ang", None),
        P(),
        P(),
        P(("chain", "dist")),
        P(),
        P(("chain", "ang", "dist"), None),
        P(("chain", "ang", "dist"), None, None),
        P(("chain", "ang", "dist"), None, None),
        P(("chain", "ang", "dist"), None, None, None),
        P(("chain", "ang", "dist"), None, None, None),
    )
    out_specs = P(("chain", "dist"), "ang", None)
    return jax.shard_map(
        functools.partial(per_device, mesh.shape["ang"], mesh.shape["dist"]),
        mesh=mesh, in_specs=in_specs, out_specs=out_specs, check_vma=False
    )
```
